128 devices in a mesh: ctx: 8 (over x, core), grp: 16 (over y, z).
Axes of the slice: x: 4, y: 4, z: 4, core: 2. Of those that a mesh axis runs over, the one named last changes fastest.
Arguments:
- queries: float32 [16, 2048, 16, 128], P('grp', 'ctx'), may hold values from -6 to 6
- key_vecs: float32 [16, 2048, 16, 128], P('grp', 'ctx'), may hold values from -6 to 6
- val_vecs: float32 [16, 2048, 32, 128], P('grp', 'ctx'), may hold values from -6 to 6
- out_gate: float32 [16, 2048, 32, 128], P('grp', 'ctx'), may hold values from -6 to 6
- log_decay: float32 [16, 32, 2048], P('grp', None, 'ctx'), may hold values from -0.8 to 0
- beta_gate: float32 [16, 32, 2048], P('grp', None, 'ctx'), may hold values from 0.1 to 0.9
- norm_gain: float32 [128], replicated, may hold values from 0.25 to 1.75
- lengths: int32 [16, 4], P('grp'), may hold values from 1 to 1024, 2048 in all within a row
- owner_slot: int32 [64], replicated, may hold values from 0 to 63, each once
Outputs:
- attn_out: float32 [16, 2048, 32, 128], P('grp', 'ctx')
- decode_states: float32 [64, 32, 128, 128], P('grp', 'ctx')
The draws below stay inside these ranges and needn't reach their ends.
Inputs may be any that keep to these rules, and one draw needn't show every extreme that they name: Each group's 4 prompt lengths sum to 2048; the longest is exactly 1024. `owner_slot`: a permutation of the 64 decode slots.
All inputs are finite; a program needn't handle non-finite values.
Results may differ from the reference program's by a relative error of at most 0.0003.
Values sent between devices are 32-bit elements; how exact they have to be, the bound alone decides.
A program may use at most 256 MiB of HBM per device.

```python
import math
import jax
import jax.numpy as jnp
import numpy as np
from jax import lax

DK = 128
DV = 128
H = 32
HK = 16
CH = 64
REQS = 4
TOK_DEV = 256
GROUP_TOKENS = 2048
PROMPT_GROUPS = 16
NREQ = 64


def draw_log_decay(key, part):
    key = jax.random.fold_in(key, 7)
    decay_rate_key, noise_random_key, segment_random_key, spike_random_key, amplitude_random_key = jax.random.split(key, 5)
    logarithm_decay_rate = jax.random.uniform(decay_rate_key, (PROMPT_GROUPS, H, 1), jnp.float32, math.log(0.5 / GROUP_TOKENS), math.log(1.0 / 30.0))
    random_noise = jax.random.uniform(noise_random_key, (PROMPT_GROUPS, H, GROUP_TOKENS), jnp.float32, 0.5, 1.5)
    segment_factor = jnp.exp(jax.random.uniform(segment_random_key, (PROMPT_GROUPS, 1, GROUP_TOKENS // TOK_DEV, 1), jnp.float32, -0.7, 0.7))
    segment_factor = jnp.broadcast_to(segment_factor, (PROMPT_GROUPS, 1, GROUP_TOKENS // TOK_DEV, TOK_DEV)).reshape(PROMPT_GROUPS, 1, GROUP_TOKENS)
    spike_active = (jax.random.uniform(spike_random_key, (PROMPT_GROUPS, 1, GROUP_TOKENS), jnp.float32) < 3.0 / GROUP_TOKENS).astype(jnp.float32)
    spike_amplitude = jax.random.uniform(amplitude_random_key, (PROMPT_GROUPS, 1, GROUP_TOKENS), jnp.float32, 0.22, 0.69)
    return (-(jnp.exp(logarithm_decay_rate) * random_noise * segment_factor) - spike_active * spike_amplitude).astype(jnp.float32)


def block_levels(key, extent, cuts, least, high):
    loudness = 1.0
    for axis_at, parts in cuts:
        draws = jax.random.uniform(jax.random.fold_in(jax.random.fold_in(key, 6), axis_at), (parts,), jnp.float32, least / len(cuts), high / len(cuts))
        loudness = loudness * jnp.repeat(jnp.exp(draws), extent[axis_at] // parts).reshape((-1,) + (1,) * (len(extent) - 1 - axis_at))
    return loudness


def split_up(amount, total, reach, slope):
    weights = [(1 << 20) // math.isqrt(standing ** slope) + 1 for standing in range(2, amount + 1)]
    spare, holding = total - reach - (amount - 1), [1] * (amount - 1)
    while spare > 0:
        movable = [i for i in range(amount - 1) if holding[i] < reach]
        whole, left = sum([weights[i] for i in movable]), spare
        for i in movable:
            extra = min(reach - holding[i], max(1, left * weights[i] // whole), spare)
            holding[i] = holding[i] + extra
            spare = spare - extra
    return np.array([reach] + holding)


def ragged(own_key, count, total, most, lean):
    if count == 2:
        one = jax.random.randint(own_key, (), max(1, total - most), min(most, total - 1) + 1)
        return jnp.stack([one, total - one])
    sizes = jnp.asarray(split_up(count, total, most, lean), jnp.int32)
    pairs = (count - 1) // 2
    donor, taker = sizes[1:1 + 2 * pairs:2], sizes[2:2 + 2 * pairs:2]
    slack = jnp.minimum(donor - 1, most - taker)
    moved = jax.random.randint(jax.random.fold_in(own_key, 1), (pairs,), 0, 1 << 20) % (slack + 1)
    sizes = sizes.at[1:1 + 2 * pairs:2].set(donor - moved).at[2:2 + 2 * pairs:2].set(taker + moved)
    return sizes[jax.random.permutation(jax.random.fold_in(own_key, 2), count)]


def noise(stream_key, dims, width, most, cuts=(), kind=jnp.bfloat16):
    array = jax.random.normal(stream_key, dims, jnp.float32) * width
    if len(cuts) > 0:
        array = block_levels(stream_key, dims, cuts, -0.22, 0.18) * array
    return jnp.clip(array, min=-most, max=most).astype(kind)


def setup_inputs(seed: int = 0) -> dict:
    key_of = jax.random.split(jax.random.key(seed), 10)
    queries = noise(key_of[0], (PROMPT_GROUPS, GROUP_TOKENS, HK, DK), 1.0, 6.0, ((0, 16), (1, 8)), jnp.float32)
    key_vecs = noise(key_of[1], (PROMPT_GROUPS, GROUP_TOKENS, HK, DK), 1.0, 6.0, ((0, 16), (1, 8)), jnp.float32)
    val_vecs = noise(key_of[2], (PROMPT_GROUPS, GROUP_TOKENS, H, DV), 1.0, 6.0, ((0, 16), (1, 8)), jnp.float32)
    out_gate = noise(key_of[3], (PROMPT_GROUPS, GROUP_TOKENS, H, DV), 1.0, 6.0, ((0, 16), (1, 8)), jnp.float32)
    log_decay = draw_log_decay(jax.random.fold_in(key_of[9], 71), 0)
    beta_gate = jnp.clip(0.1 + 0.79999997 * jax.random.uniform(key_of[5], (PROMPT_GROUPS, H, GROUP_TOKENS), jnp.float32) ** block_levels(key_of[5], (PROMPT_GROUPS, H, GROUP_TOKENS), ((0, 16), (2, 8)), -0.2, 0.2), 0.1, 0.9)
    norm_gain = jnp.clip(1.0 + 0.15 * jax.random.normal(key_of[6], (DV,), jnp.float32), 0.25, 1.75)
    lengths = jax.vmap(lambda own: ragged(own, REQS, GROUP_TOKENS, GROUP_TOKENS // 2, 2))(jax.random.split(key_of[7], PROMPT_GROUPS)).reshape((PROMPT_GROUPS, REQS)).astype(jnp.int32)
    owner_slot = jax.random.permutation(key_of[8], NREQ).astype(jnp.int32)
    return {"queries": queries, "key_vecs": key_vecs, "val_vecs": val_vecs, "out_gate": out_gate, "log_decay": log_decay, "beta_gate": beta_gate, "norm_gain": norm_gain, "lengths": lengths, "owner_slot": owner_slot}


exact_mode = lax.Precision.HIGHEST

def unit_norm(vectors):
    return vectors / jnp.sqrt(lax.optimization_barrier(jnp.sum(vectors * vectors, axis=-1, keepdims=True)) + 1e-06)

def batch_mm(left_mat, right_mat):
    return jnp.einsum('...ij,...jk->...ik', left_mat, right_mat, precision=exact_mode)

def span_terms(query_blk, key_blk, value_blk, decay_blk, beta_blk, segment_blk, carry_mask):
    block_len = query_blk.shape[-2]
    key_dim = key_blk.shape[-1]
    value_dim = value_blk.shape[-1]
    cumlog = jnp.cumsum(decay_blk, axis=-1)
    log_diffs = cumlog[..., :, None] - cumlog[..., None, :]
    row_ids = lax.broadcasted_iota(jnp.int32, (block_len, block_len), 0)
    col_ids = lax.broadcasted_iota(jnp.int32, (block_len, block_len), 1)
    same_seg = segment_blk[..., :, None] == segment_blk[..., None, :]
    inclusive = same_seg & (col_ids <= row_ids)
    strictly = same_seg & (col_ids < row_ids)
    decay_in = jnp.where(inclusive, jnp.exp(jnp.where(inclusive, log_diffs, 0.0)), 0.0)
    decay_st = jnp.where(strictly, decay_in, 0.0)
    key_gram = jnp.einsum('...id,...jd->...ij', key_blk, key_blk, precision=exact_mode)
    lower_part = beta_blk[..., :, None] * key_gram * decay_st
    identity = jnp.eye(block_len, dtype=decay_in.dtype)
    gamma_vec = jnp.exp(cumlog) * carry_mask
    rhs_all = jnp.concatenate([beta_blk[..., None] * value_blk, (beta_blk * gamma_vec)[..., None] * key_blk], axis=-1)
    system_mat = jnp.broadcast_to(identity + lower_part, lower_part.shape)
    solved = lax.linalg.triangular_solve(system_mat, rhs_all, left_side=True, lower=True, unit_diagonal=True)
    upd_base = solved[..., :value_dim]
    write_keys = solved[..., value_dim:]
    scores = jnp.einsum('...id,...jd->...ij', query_blk, key_blk, precision=exact_mode) * decay_in
    out_base = batch_mm(scores, upd_base)
    query_eff = gamma_vec[..., None] * query_blk - batch_mm(scores, write_keys)
    tail_keys = decay_in[..., -1, :][..., None] * key_blk
    eye_key = jnp.eye(key_dim, dtype=decay_in.dtype)
    transition = gamma_vec[..., -1][..., None, None] * eye_key - jnp.einsum('...jd,...je->...de', write_keys, tail_keys, precision=exact_mode)
    bias_term = jnp.einsum('...jv,...jd->...vd', upd_base, tail_keys, precision=exact_mode)
    return (out_base, query_eff, write_keys, upd_base, transition, bias_term, decay_in, gamma_vec)

def reference(queries, key_vecs, val_vecs, out_gate, log_decay, beta_gate, norm_gain, lengths, owner_slot):
    seq_ends = jnp.cumsum(lengths, axis=1).astype(jnp.int32)
    seq_starts = seq_ends - lengths
    positions = jnp.arange(GROUP_TOKENS, dtype=jnp.int32)
    segment = lax.optimization_barrier(jnp.sum((positions[None, :, None] >= seq_ends[:, None, :]).astype(jnp.int32), axis=2))
    is_first = lax.optimization_barrier(jnp.sum((positions[None, :, None] == seq_starts[:, None, :]).astype(jnp.int32), axis=2))
    group_rep = H // HK
    q_scale = DK ** (-0.5)

    def advance(carry_val, block_idx):
        run_state, finals = carry_val
        block_lo = block_idx * CH
        query_blk = unit_norm(lax.dynamic_slice_in_dim(queries, block_lo, CH, 1)) * q_scale
        key_blk = unit_norm(lax.dynamic_slice_in_dim(key_vecs, block_lo, CH, 1))
        query_blk = jnp.repeat(query_blk, group_rep, axis=2).transpose(0, 2, 1, 3)
        key_blk = jnp.repeat(key_blk, group_rep, axis=2).transpose(0, 2, 1, 3)
        value_blk = lax.dynamic_slice_in_dim(val_vecs, block_lo, CH, 1).transpose(0, 2, 1, 3)
        decay_blk = lax.dynamic_slice_in_dim(log_decay, block_lo, CH, 2)
        beta_blk = lax.dynamic_slice_in_dim(beta_gate, block_lo, CH, 2)
        segment_blk = lax.dynamic_slice_in_dim(segment, block_lo, CH, 1)[:, None, :]
        first_blk = lax.dynamic_slice_in_dim(is_first, block_lo, CH, 1)
        carry_mask = (jnp.cumsum(first_blk, axis=1) == 0).astype(decay_blk.dtype)[:, None, :]
        out_base, query_eff, write_keys, upd_base, transition, bias_term, decay_in, gamma_vec = span_terms(query_blk, key_blk, value_blk, decay_blk, beta_blk, segment_blk, carry_mask)
        out_blk = out_base + jnp.einsum('ghid,ghvd->ghiv', query_eff, run_state, precision=exact_mode)
        upd_blk = upd_base - jnp.einsum('ghid,ghvd->ghiv', write_keys, run_state, precision=exact_mode)
        end_pick = ((seq_ends - 1)[:, :, None] == block_lo + jnp.arange(CH, dtype=jnp.int32)[None, None, :]).astype(decay_blk.dtype)
        weights = jnp.einsum('gri,ghij->ghrj', end_pick, decay_in, precision=exact_mode)
        amplitude = jnp.einsum('gri,ghi->grh', end_pick, gamma_vec, precision=exact_mode)
        weighted = weights[..., None] * upd_blk[:, :, None, :, :]
        finals = finals + amplitude[..., None, None] * run_state[:, None] + jnp.einsum('ghrjv,ghjd->grhvd', weighted, key_blk, precision=exact_mode)
        run_state = batch_mm(run_state, transition) + bias_term
        return ((run_state, finals), out_blk)
    start_state = jnp.zeros((PROMPT_GROUPS, H, DV, DK), jnp.float32)
    start_finals = jnp.zeros((PROMPT_GROUPS, REQS, H, DV, DK), jnp.float32)
    block_ids = jnp.arange(GROUP_TOKENS // CH, dtype=jnp.int32)
    (last_state, finals), out_blocks = lax.scan(advance, (start_state, start_finals), block_ids)
    raw_out = out_blocks.transpose(1, 0, 3, 2, 4).reshape(PROMPT_GROUPS, GROUP_TOKENS, H, DV)
    mean_sq = lax.optimization_barrier(jnp.mean(raw_out * raw_out, axis=-1, keepdims=True))
    attn_out = raw_out / jnp.sqrt(mean_sq + 1e-06) * norm_gain * jax.nn.silu(out_gate)
    decode_states = jnp.zeros((NREQ, H, DV, DK), jnp.float32).at[owner_slot].set(finals.reshape(NREQ, H, DV, DK))
    return (attn_out, decode_states)
```

```python
import jax
import jax.numpy as jnp
from jax import lax
from jax.experimental import pallas as pl
from jax.experimental.pallas import tpu as pltpu
from jax.sharding import PartitionSpec as P

CH = 64
D = 128
HK = 16
H = 32
TOK = 256
NC = TOK // CH
REQS = 4
F32 = jnp.float32
BF16 = jnp.bfloat16
MESH = pl.DeviceIdType.MESH
VMEM = pl.BlockSpec(memory_space=pltpu.VMEM)
SMEM = pl.BlockSpec(memory_space=pltpu.SMEM)


def mm(x, y):
    return lax.dot_general(x, y, (((1,), (0,)), ((), ())), preferred_element_type=F32)


def split(x):
    hi = x.astype(BF16)
    return hi, (x - hi.astype(F32)).astype(BF16)


def dot_wide(x, y):
    xh, xl = split(x)
    yh, yl = split(y)
    left = jnp.concatenate([xh, xl], axis=1)
    return mm(left, jnp.concatenate([yh, yh], axis=0)) + mm(xh, yl)


def dot_twin(x, y):
    low = x - x.astype(BF16).astype(F32)
    lane = lax.broadcasted_iota(jnp.int32, x.shape, 1)
    s = jnp.where(lane < CH, x, low).astype(BF16)
    yh, yl = split(y)
    left = jnp.concatenate([s, s], axis=1)
    return mm(left, jnp.concatenate([yh, yh, yl, yl], axis=0))


def prompt_ends(len_ref):
    ends = [len_ref[0, 0]]
    for r in range(1, REQS):
        ends.append(ends[-1] + len_ref[0, r])
    return ends


def seg_start(pos, ends):
    start = jnp.zeros(pos.shape, jnp.int32)
    for e in ends[:-1]:
        start = jnp.where(pos >= e, e, start)
    return start


def terms_kernel(
    len_ref, q_ref, k_ref, v_ref, ld_ref, be_ref,
    out0_ref, qe_ref, m1_ref, b1_ref, bo_ref, f0_ref, flag_ref,
    kn_s, qn_s, kt_s, gram_s, qk_s, low_s, inv_s, t_s,
    cum_s, gam_s, cumt_s, gamt_s, bet_s, start_s, bias_s, col_s, gcol_s, st_s, u_s,
):
    off = lax.axis_index("ctx") * TOK
    ends = prompt_ends(len_ref)
    lane = lax.broadcasted_iota(jnp.int32, (D, D), 1)
    row = lax.broadcasted_iota(jnp.int32, (D, D), 0)

    cum = ld_ref[...]
    tok = lane % CH
    for s in (1, 2, 4, 8, 16, 32):
        cum = cum + jnp.where(tok >= s, pltpu.roll(cum, s, 1), 0.0)
    lo_a = off + (row % NC) * CH
    carry_a = seg_start(lo_a + tok, ends) < lo_a
    gam = jnp.where(carry_a, jnp.exp(cum), 0.0)
    cum_s[...] = cum
    gam_s[...] = gam
    cumt_s[...] = cum.T[:CH]
    gamt_s[...] = gam.T[:CH]
    bet_s[...] = be_ref[...].T[:CH]
    lane_b = lane[:CH]
    row_b = row[:CH]
    start_s[...] = seg_start(off + (lane_b % NC) * CH + row_b, ends)
    tok_b = tok[:CH]
    for c in range(NC):
        lo = off + c * CH
        same = seg_start(lo + row_b, ends) == seg_start(lo + tok_b, ends)
        bias_s[pl.ds(c * CH, CH), :] = jnp.where(same & (tok_b <= row_b), 0.0, -1e30)

    @pl.loop(0, 8)
    def _(i):
        for u in range(16):
            f0_ref[i, u] = jnp.zeros((D, D), F32)

    @pl.loop(0, HK)
    def _(hk):
        k = k_ref[pl.ds(hk, TOK, stride=HK), :]
        q = q_ref[pl.ds(hk, TOK, stride=HK), :]
        kn = k * lax.rsqrt(jnp.sum(k * k, axis=1, keepdims=True) + 1e-6)
        qn = q * (lax.rsqrt(jnp.sum(q * q, axis=1, keepdims=True) + 1e-6) * (D**-0.5))
        kn_s[hk] = kn
        qn_s[hk] = qn
        for c in range(NC):
            kc = kn[c * CH : (c + 1) * CH]
            qc = qn[c * CH : (c + 1) * CH]
            kt = jnp.concatenate([kc, kc], axis=0).T
            kt_s[hk * NC + c] = kt
            g = dot_wide(jnp.concatenate([kc, qc], axis=0), kt)
            gram_s[pl.ds((hk * NC + c) * CH, CH), :] = g[:CH]
            qk_s[hk * NC + c] = g[CH:]

    @pl.loop(0, CH)
    def _(i):
        x = gram_s[pl.ds(i, HK * NC, stride=CH), :]
        xt = jnp.concatenate([x, x], axis=0).T[:CH]
        keep = (start_s[...] == start_s[pl.ds(i, 1), :]) & (row_b < i)
        decay = jnp.exp(jnp.where(keep, cumt_s[pl.ds(i, 1), :] - cumt_s[...], -1e30))
        low_s[pl.ds(i * CH, CH), :] = xt * decay * bet_s[pl.ds(i, 1), :]

    for g in range(CH // 4):
        n = 8 * ((4 * g + 3) // 8 + 1)
        rid = lax.broadcasted_iota(jnp.int32, (n, D), 0)
        acc = tuple(jnp.where(rid == 4 * g + a, 1.0, 0.0).astype(F32) for a in range(4))

        def body(jb, acc, g=g, n=n):
            acc = list(acc)
            for b in range(4):
                t = inv_s[pl.ds((jb * 4 + b) * CH, n), :]
                for a in range(4):
                    acc[a] = acc[a] - low_s[pl.ds((4 * g + a) * CH + jb * 4 + b, 1), :] * t
            return tuple(acc)

        if g:
            acc = lax.fori_loop(0, g, body, acc)
        acc = list(acc)
        for a in range(4):
            for b in range(a):
                acc[a] = acc[a] - low_s[pl.ds((4 * g + a) * CH + 4 * g + b, 1), :] * acc[b]
            inv_s[pl.ds((4 * g + a) * CH, n), :] = acc[a]
            if n < CH:
                inv_s[pl.ds((4 * g + a) * CH + n, CH - n), :] = jnp.zeros((CH - n, D), F32)

    @pl.loop(0, CH)
    def _(i):
        x = inv_s[pl.ds(i * CH, CH), :] * bet_s[...]
        t_s[pl.ds(i, D, stride=CH), :] = jnp.concatenate([x, x], axis=0).T

    first_end = ends[-1]
    for e in ends[-2::-1]:
        first_end = jnp.where(e > off, e, first_end)
    marks = [first_end >= off + TOK]
    begin = 0
    for e in ends:
        marks.append((begin <= off) & (e > off) & (e <= off + TOK))
        begin = e
    mark = jnp.zeros((8, D), F32)
    for i, m in enumerate(marks):
        mark = jnp.where(row[:8] == i, jnp.where(m, 1.0, 0.0), mark)
    flag_ref[...] = mark

    eye = jnp.where(lane == row, 1.0, 0.0).astype(F32)
    zero = jnp.zeros((CH, D), F32)

    @pl.loop(0, HK)
    def _(hk):
        shift = lax.rem(D - hk * NC, D)
        col_s[...] = pltpu.roll(cumt_s[...], shift, 1)
        gcol_s[...] = pltpu.roll(gamt_s[...], shift, 1)
        col = col_s[...]
        gcol = gcol_s[...]
        state = [jnp.concatenate([jnp.zeros((D, D), F32), eye], axis=1) for _ in range(2)]
        for c in range(NC):
            kc = kn_s[hk, pl.ds(c * CH, CH), :]
            qc = qn_s[hk, pl.ds(c * CH, CH), :]
            kt = kt_s[hk * NC + c]
            qk = qk_s[hk * NC + c]
            bias = bias_s[pl.ds(c * CH, CH), :]
            for r in range(2):
                at = r * CH + c
                b = r * CH + hk * NC + c
                ccol = col[:, at : at + 1]
                gc = gcol[:, at : at + 1]
                decay = jnp.exp(ccol - cum_s[pl.ds(b, 1), :] + bias)
                v = v_ref[pl.ds(c * CH * H + hk * 2 + r, CH, stride=H), :]
                gq = qc * gc
                uw = dot_twin(t_s[pl.ds(b * CH, CH), :], jnp.concatenate([v, kc * gc], axis=1))
                u0, w = uw[:, :D], uw[:, D:]
                if c == 0:
                    u = jnp.concatenate([u0, -w], axis=1)
                    base = jnp.concatenate([zero, gq], axis=1)
                else:
                    p = dot_wide(jnp.concatenate([w, gq], axis=0), state[r])
                    u = jnp.concatenate([u0, zero], axis=1) - p[:CH]
                    base = p[CH:]
                left = jnp.concatenate([qk * decay, kt * decay[CH - 1 : CH]], axis=0)
                res = dot_twin(left, u)
                o = base + res[:CH]
                h = hk * 2 + r
                out0_ref[h, pl.ds(c * CH, CH), :] = o[:, :D]
                qe_ref[h, pl.ds(c * CH, CH), :] = o[:, D:]
                st_s[r, c] = state[r]
                u_s[r, c] = u
                state[r] = gc[CH - 1 : CH] * state[r] + res[CH:]
        for r in range(2):
            h = hk * 2 + r
            bo_ref[h] = state[r][:, :D]
            b1_ref[h] = state[r][:, :D]
            m1_ref[h] = state[r][:, D:]
        begin = 0
        for p in range(REQS):
            last = ends[p] - 1 - off
            opens = begin <= off
            begin = ends[p]

            @pl.when((last >= 0) & (last < TOK))
            def _(last=last, opens=opens, p=p):
                c = last // CH
                e = last % CH
                for r in range(2):
                    h = hk * 2 + r
                    at = lane[:1] == r * CH + c
                    crow = cum_s[pl.ds(r * CH + hk * NC + c, 1), :]
                    cume = jnp.sum(jnp.where(at, col_s[pl.ds(e, 1), :], 0.0), axis=1, keepdims=True)
                    amp = jnp.sum(jnp.where(at, gcol_s[pl.ds(e, 1), :], 0.0), axis=1, keepdims=True)
                    drow = jnp.exp(cume - crow + bias_s[pl.ds(c * CH + e, 1), :])
                    f = amp * st_s[r, c] + dot_twin(kt_s[hk * NC + c] * drow, u_s[r, c])

                    @pl.when(opens)
                    def _():
                        b1_ref[h] = f[:, :D]
                        m1_ref[h] = f[:, D:]

                    @pl.when(jnp.logical_not(opens))
                    def _():
                        unit = lax.rem(hk, 2) * 8 + p * 2 + r
                        f0_ref[lax.rem(hk // 2, 2) * 4 + hk // 4, unit] = f[:, :D].T


def local_terms(lengths, q, k, v, ld, be):
    hm = jax.ShapeDtypeStruct((H, D, D), F32)
    tokens = jax.ShapeDtypeStruct((H, TOK, D), F32)
    vm = pltpu.VMEM
    return pl.pallas_call(
        terms_kernel,
        out_shape=(
            tokens, tokens, hm, hm, hm,
            jax.ShapeDtypeStruct((8, 16, D, D), F32),
            jax.ShapeDtypeStruct((8, D), F32),
        ),
        in_specs=[SMEM] + [VMEM] * 5,
        out_specs=tuple([VMEM] * 7),
        scratch_shapes=[
            vm((HK, TOK, D), F32),
            vm((HK, TOK, D), F32),
            vm((HK * NC, D, D), F32),
            vm((HK * NC * CH, D), F32),
            vm((HK * NC, CH, D), F32),
            vm((CH * CH, D), F32),
            vm((CH * CH, D), F32),
            vm((D * CH, D), F32),
            vm((D, D), F32),
            vm((D, D), F32),
            vm((CH, D), F32),
            vm((CH, D), F32),
            vm((CH, D), F32),
            vm((CH, D), jnp.int32),
            vm((TOK, D), F32),
            vm((CH, D), F32),
            vm((CH, D), F32),
            vm((2, NC, D, 2 * D), F32),
            vm((2, NC, CH, 2 * D), F32),
        ],
        compiler_params=pltpu.CompilerParams(vmem_limit_bytes=60 * 1024 * 1024),
        name="local_terms",
    )(lengths, q, k, v, ld, be)


def lines(me_ctx, me_grp):
    y, z = me_grp // 4, lax.rem(me_grp, 4)
    core = lax.rem(me_ctx, 2)

    def turn(i, by):
        return lax.rem(i + by, 4)

    return dict(
        twin={"ctx": me_ctx + 1 - 2 * core},
        chain={"ctx": lax.rem(me_ctx + 7 + 2 * core, 8)},
        x=({"ctx": lax.rem(me_ctx + 2, 8)}, {"ctx": lax.rem(me_ctx + 6, 8)}),
        z=({"grp": y * 4 + turn(z, 1)}, {"grp": y * 4 + turn(z, 3)}),
        y=({"grp": turn(y, 1) * 4 + z}, {"grp": turn(y, 3) * 4 + z}),
    )


class Copies:
    def __init__(self, send_sem, recv_sem):
        self.send_sem, self.recv_sem, self.made = send_sem, recv_sem, []

    def start(self, src, dst, device):
        i = len(self.made)
        made = pltpu.make_async_remote_copy(
            src_ref=src,
            dst_ref=dst,
            send_sem=self.send_sem.at[i],
            recv_sem=self.recv_sem.at[i],
            device_id=device,
            device_id_type=MESH,
        )
        made.start()
        self.made.append(made)
        return made

    def finish(self):
        for made in self.made:
            made.wait_send()


def add_units(dst, at, lo, n, src):
    @pl.loop(0, n)
    def _(u):
        dst[at, lo + u] = dst[at, lo + u] + src[u]


def sum_ring_begin(copies, buf, m, pos, pair, ra, rb, rc, rd):
    nxt, opp, prv = (lax.rem(pos + i, 4) for i in (1, 2, 3))
    up, down = pair
    c0 = copies.start(buf.at[opp, pl.ds(0, m)], ra, up)
    c1 = copies.start(buf.at[opp, pl.ds(m, m)], rb, down)
    c2 = copies.start(buf.at[nxt, pl.ds(m, m)], rc.at[pl.ds(m, m)], up)
    c3 = copies.start(buf.at[prv, pl.ds(0, m)], rd.at[pl.ds(0, m)], down)
    return c0, c1, c2, c3


def sum_ring_pass(copies, buf, m, pos, pair, ra, rb, rc, rd, begun):
    nxt, prv = lax.rem(pos + 1, 4), lax.rem(pos + 3, 4)
    up, down = pair
    c0, c1, c2, c3 = begun
    c0.wait_recv()
    add_units(buf, nxt, 0, m, ra)
    c4 = copies.start(buf.at[nxt, pl.ds(0, m)], rc.at[pl.ds(0, m)], up)
    c1.wait_recv()
    add_units(buf, prv, m, m, rb)
    c5 = copies.start(buf.at[prv, pl.ds(m, m)], rd.at[pl.ds(m, m)], down)
    return c2, c3, c4, c5


def chain_kernel(
    idx_ref, m_ref, b1_ref, bo_ref, flag_ref, f0_ref, in_ref, dec_ref,
    out_s, end_s, twin_s, xa, xb, xc, xd, got_a, got_b, put_s, ya, yb, yc, yd,
    chain_send, chain_recv, send_sem, recv_sem,
):
    me = lax.axis_index("ctx")
    grp = lax.axis_index("grp")
    core, chip = lax.rem(me, 2), me // 2
    at = lines(me, grp)
    barrier = pltpu.get_barrier_semaphore()
    for device in (at["twin"], at["chain"], *at["x"], *at["y"], *at["z"]):
        pl.semaphore_signal(barrier, inc=1, device_id=device, device_id_type=MESH)
    pl.semaphore_wait(barrier, 8)
    copies = Copies(send_sem, recv_sem)
    got_s = (got_a, got_b)

    def pass_on(h):
        return pltpu.make_async_remote_copy(
            src_ref=out_s.at[h],
            dst_ref=in_ref.at[h],
            send_sem=chain_send.at[h],
            recv_sem=chain_recv.at[h],
            device_id={"ctx": lax.rem(me + 1, 8)},
            device_id_type=MESH,
        )

    @pl.when(me == 0)
    def _():
        @pl.loop(0, H)
        def _(h):
            in_ref[h] = jnp.zeros((D, D), F32)

    twins = []
    for c in range(4):

        @pl.loop(0, 8)
        def _(j, c=c):
            h = c * 8 + j

            @pl.when(me > 0)
            def _():
                pass_on(h).wait_recv()

            x = dot_wide(m_ref[h], in_ref[h])
            out_s[h] = x * flag_ref[0:1, :] + bo_ref[h]

            @pl.when(me < 7)
            def _():
                pass_on(h).start()

            xt = (x + b1_ref[h]).T
            k, unit = j // 4, (lax.rem(j, 4) // 2) * 8 + lax.rem(j, 2)
            for p in range(REQS):
                here = flag_ref[1 + p : 2 + p, :]
                end_s[k * 4 + c, unit + 2 * p] = f0_ref[k * 4 + c, unit + 2 * p] + here * xt

        twins.append(copies.start(end_s.at[(1 - core) * 4 + c], twin_s.at[c], at["twin"]))

    for c in range(4):
        twins[c].wait_recv()

        @pl.loop(0, 16)
        def _(u, c=c):
            twin_s[c, u] = twin_s[c, u] + end_s[core * 4 + c, u]

    bufs = (xa, xb, xc, xd)
    begun = sum_ring_begin(copies, twin_s, 8, chip, at["x"], *bufs)
    rest = sum_ring_pass(copies, twin_s, 8, chip, at["x"], *bufs, begun)
    for made in rest:
        made.wait_recv()
    y, z = grp // 4, lax.rem(grp, 4)
    places = ((z, at["z"], y, at["y"]), (y, at["y"], z, at["z"]))

    for half, (pos, _pair, _, _) in enumerate(places):

        @pl.loop(0, 8)
        def _(u, half=half, pos=pos):
            i = half * 8 + u
            got_s[half][pos * 8 + u] = twin_s[chip, i] + xc[i] + xd[i]

    direct = []
    for half, (pos, pair, _, _) in enumerate(places):
        mine = got_s[half].at[pl.ds(pos * 8, 8)]
        direct.append((copies.start(mine, mine, pair[0]), copies.start(mine, mine, pair[1])))
    onward = []
    for half, (pos, pair, _, _) in enumerate(places):
        nxt, prv = lax.rem(pos + 1, 4), lax.rem(pos + 3, 4)
        direct[half][0].wait_recv()
        part = got_s[half].at[pl.ds(prv * 8, 4)]
        c0 = copies.start(part, part, pair[0])
        direct[half][1].wait_recv()
        part = got_s[half].at[pl.ds(nxt * 8 + 4, 4)]
        c1 = copies.start(part, part, pair[1])
        onward.append((c0, c1))
    begun = []
    for half, (_, _, pos, pair) in enumerate(places):
        onward[half][0].wait_recv()
        onward[half][1].wait_recv()

        @pl.loop(0, 16)
        def _(i, half=half):
            src = idx_ref[half, i]
            for h2 in range(2):
                x = got_s[half][jnp.maximum(src, 0) * 2 + h2]
                put_s[half * 4 + i // 4, lax.rem(i, 4) * 2 + h2] = jnp.where(src >= 0, x, 0.0)

        bufs = tuple(b.at[half] for b in (ya, yb, yc, yd))
        put = put_s.at[pl.ds(half * 4, 4)]
        begun.append(sum_ring_begin(copies, put, 4, pos, pair, *bufs))
    rest = []
    for half, (_, _, pos, pair) in enumerate(places):
        bufs = tuple(b.at[half] for b in (ya, yb, yc, yd))
        put = put_s.at[pl.ds(half * 4, 4)]
        rest.append(sum_ring_pass(copies, put, 4, pos, pair, *bufs, begun[half]))
    for half, (_, _, pos, pair) in enumerate(places):
        for made in rest[half]:
            made.wait_recv()

        @pl.loop(0, 8)
        def _(u, half=half, pos=pos):
            x = put_s[half * 4 + pos, u] + yc[half, u] + yd[half, u]
            dec_ref[u // 2, half * 2 + lax.rem(u, 2)] = x

    @pl.when(me < 7)
    def _():
        @pl.loop(0, H)
        def _(h):
            pass_on(h).wait_send()

    copies.finish()


def chain(idx, m1, b1, bo, flag, f0):
    vm = pltpu.VMEM

    def units(*n):
        return vm(n + (D, D), F32)

    return pl.pallas_call(
        chain_kernel,
        out_shape=(
            jax.ShapeDtypeStruct((H, D, D), F32),
            jax.ShapeDtypeStruct((REQS, REQS, D, D), F32),
        ),
        in_specs=[SMEM] + [VMEM] * 5,
        out_specs=(VMEM, VMEM),
        scratch_shapes=[
            units(H), units(8, 16), units(4, 16),
            units(8), units(8), units(16), units(16),
            units(32), units(32), units(8, 8),
            units(2, 4), units(2, 4), units(2, 8), units(2, 8),
            pltpu.SemaphoreType.DMA((H,)),
            pltpu.SemaphoreType.DMA((H,)),
            pltpu.SemaphoreType.DMA((32,)),
            pltpu.SemaphoreType.DMA((32,)),
        ],
        compiler_params=pltpu.CompilerParams(
            collective_id=0, has_side_effects=True, vmem_limit_bytes=60 * 1024 * 1024
        ),
        name="state_chain",
    )(idx, m1, b1, bo, flag, f0)


HB = 8


def gate_kernel(out0_ref, qe_ref, x_ref, gate_ref, gain_ref, o_ref):
    gain = gain_ref[...]
    gate = gate_ref.reshape(TOK * HB, D)
    dst = o_ref.reshape(TOK * HB, D)
    for h in range(HB):
        raw = out0_ref[h] + dot_wide(qe_ref[h], x_ref[h])
        ms = jnp.sum(raw * raw, axis=1, keepdims=True) * (1.0 / D)
        g = gate[pl.ds(h, TOK, stride=HB), :]
        act = g / (1.0 + jnp.exp(-g))
        dst[pl.ds(h, TOK, stride=HB), :] = raw * lax.rsqrt(ms + 1e-6) * gain * act


def gated_out(out0, qe, x_in, gate, gain):
    tok = pl.BlockSpec((HB, TOK, D), lambda i: (i, 0, 0))
    nat = pl.BlockSpec((TOK, HB, D), lambda i: (0, i, 0))
    return pl.pallas_call(
        gate_kernel,
        grid=(H // HB,),
        out_shape=jax.ShapeDtypeStruct((TOK, H, D), F32),
        in_specs=[
            tok, tok,
            pl.BlockSpec((HB, D, D), lambda i: (i, 0, 0)),
            nat,
            pl.BlockSpec((1, D), lambda i: (0, 0)),
        ],
        out_specs=nat,
        compiler_params=pltpu.CompilerParams(vmem_limit_bytes=40 * 1024 * 1024),
        cost_estimate=pl.CostEstimate(flops=800000000, bytes_accessed=20000000, transcendentals=0),
        name="gated_out",
    )(out0, qe, x_in, gate, gain)


def routes(owner_slot):
    me = lax.axis_index("grp")
    y, z = me // 4, me % 4
    other = jnp.arange(4)
    along_z, along_y = y * 4 + other, other * 4 + z
    out = []
    for sources, targets in ((along_z, along_y), (along_y, along_z)):
        slots = owner_slot.reshape(16, REQS)[sources].reshape(-1)
        wanted = (targets[:, None] * REQS + jnp.arange(REQS)[None, :]).reshape(-1)
        hit = wanted[:, None] == slots[None, :]
        out.append(jnp.max(jnp.where(hit, jnp.arange(16)[None, :], -1), axis=1))
    return jnp.stack(out).astype(jnp.int32)


def local(
    queries, key_vecs, val_vecs, out_gate, log_decay, beta_gate, norm_gain, lengths, owner_slot
):
    def rows(x):
        x = x[0].reshape(HK, 2, NC, CH).transpose(1, 0, 2, 3).reshape(D, CH)
        return jnp.concatenate([x, x], axis=1)

    out0, qe, m1, b1, bo, f0, flag = local_terms(
        lengths,
        queries.reshape(TOK * HK, D),
        key_vecs.reshape(TOK * HK, D),
        val_vecs.reshape(TOK * H, D),
        rows(log_decay),
        rows(beta_gate),
    )
    x_in, decode = chain(routes(owner_slot), m1, b1, bo, flag, f0)
    attn = gated_out(out0, qe, x_in, out_gate[0], norm_gain.reshape(1, D))
    return attn[None], decode


def solution(mesh):
    return jax.shard_map(
        local,
        mesh=mesh,
        in_specs=(
            P("grp", "ctx", None, None),
            P("grp", "ctx", None, None),
            P("grp", "ctx", None, None),
            P("grp", "ctx", None, None),
            P("grp", None, "ctx"),
            P("grp", None, "ctx"),
            P(),
            P("grp", None),
            P(),
        ),
        out_specs=(P("grp", "ctx", None, None), P("grp", "ctx", None, None)),
        check_vma=False,
    )
```

```python
import jax
import jax.numpy as jnp
from jax import lax
from jax.experimental import pallas as pl
from jax.experimental.pallas import tpu as pltpu
from jax.sharding import PartitionSpec as P

CH = 64
D = 128
HK = 16
H = 32
TOK = 256
NC = TOK // CH
REQS = 4
NI = 2
F32 = jnp.float32
BF16 = jnp.bfloat16
MESH = pl.DeviceIdType.MESH
VMEM = pl.BlockSpec(memory_space=pltpu.VMEM)
SMEM = pl.BlockSpec(memory_space=pltpu.SMEM)
ANY = pl.BlockSpec(memory_space=pl.ANY)


def mm(x, y):
    return lax.dot_general(x, y, (((1,), (0,)), ((), ())), preferred_element_type=F32)


def split(x):
    hi = x.astype(BF16)
    return hi, (x - hi.astype(F32)).astype(BF16)


def dot_wide(x, y):
    xh, xl = split(x)
    yh, yl = split(y)
    left = jnp.concatenate([xh, xl], axis=1)
    return mm(left, jnp.concatenate([yh, yh], axis=0)) + mm(xh, yl)


def dot_twin(x, y):
    low = x - x.astype(BF16).astype(F32)
    lane = lax.broadcasted_iota(jnp.int32, x.shape, 1)
    s = jnp.where(lane < CH, x, low).astype(BF16)
    yh, yl = split(y)
    left = jnp.concatenate([s, s], axis=1)
    return mm(left, jnp.concatenate([yh, yh, yl, yl], axis=0))


def prompt_ends(len_ref):
    ends = [len_ref[0, 0]]
    for r in range(1, REQS):
        ends.append(ends[-1] + len_ref[0, r])
    return ends


def seg_start(pos, ends):
    start = jnp.zeros(pos.shape, jnp.int32)
    for e in ends[:-1]:
        start = jnp.where(pos >= e, e, start)
    return start


def terms_kernel(
    len_ref, q_ref, k_ref, v_hbm, ld_ref, be_ref,
    out0_hbm, qe_hbm, m1_hbm, b1_hbm, bo_hbm, f0_hbm, flag_ref,
    out0_ref, qe_ref, m1_ref, b1_ref, bo_ref, f0_ref, v_ref, out_sem, in_sem,
    kn_s, qn_s, kt_s, gram_s, qk_s, low_s, inv_s, t_s,
    cum_s, gam_s, cumt_s, gamt_s, bet_s, start_s, bias_s, col_s, gcol_s, st_s, u_s,
):
    load_v = pltpu.make_async_copy(v_hbm, v_ref, in_sem.at[0])
    load_v.start()
    off = lax.axis_index("ctx") * TOK
    ends = prompt_ends(len_ref)
    lane = lax.broadcasted_iota(jnp.int32, (D, D), 1)
    row = lax.broadcasted_iota(jnp.int32, (D, D), 0)

    tok = lane % CH
    for i, src in enumerate((ld_ref, be_ref)):
        x = src[...]
        low_s[2 * i * H : (2 * i + 1) * H, :] = x[:, :D]
        low_s[(2 * i + 1) * H : (2 * i + 2) * H, :] = x[:, D:]
    for c in range(NC):
        for r in range(2):
            for i, dst in enumerate((cum_s, gam_s)):
                x = low_s[pl.ds((2 * i + c // 2) * H + r, HK, stride=2), :]
                y = pltpu.roll(x, CH, 1)
                x = jnp.where((lane[:HK] < CH) == (c % 2 == 0), x, y)
                dst[pl.ds(r * CH + c, HK, stride=NC), :] = x
    cum = cum_s[...]
    beta = gam_s[...]
    for s in (1, 2, 4, 8, 16, 32):
        cum = cum + jnp.where(tok >= s, pltpu.roll(cum, s, 1), 0.0)
    lo_a = off + (row % NC) * CH
    carry_a = seg_start(lo_a + tok, ends) < lo_a
    gam = jnp.where(carry_a, jnp.exp(cum), 0.0)
    cum_s[...] = cum
    gam_s[...] = gam
    cumt_s[...] = cum.T[:CH]
    gamt_s[...] = gam.T[:CH]
    bet_s[...] = beta.T[:CH]
    lane_b = lane[:CH]
    row_b = row[:CH]
    start_s[...] = seg_start(off + (lane_b % NC) * CH + row_b, ends)
    tok_b = tok[:CH]
    for c in range(NC):
        lo = off + c * CH
        same = seg_start(lo + row_b, ends) == seg_start(lo + tok_b, ends)
        bias_s[pl.ds(c * CH, CH), :] = jnp.where(same & (tok_b <= row_b), 0.0, -1e30)

    @pl.loop(0, 8)
    def _(i):
        for u in range(16):
            f0_ref[i, u // 4, u % 4] = jnp.zeros((D, D), F32)

    @pl.loop(0, HK, unroll=4)
    def _(hk):
        k = k_ref[pl.ds(hk, TOK, stride=HK), :]
        q = q_ref[pl.ds(hk, TOK, stride=HK), :]
        kn = k * lax.rsqrt(jnp.sum(k * k, axis=1, keepdims=True) + 1e-6)
        qn = q * (lax.rsqrt(jnp.sum(q * q, axis=1, keepdims=True) + 1e-6) * (D**-0.5))
        kn_s[hk] = kn
        qn_s[hk] = qn
        for c in range(NC):
            kc = kn[c * CH : (c + 1) * CH]
            qc = qn[c * CH : (c + 1) * CH]
            kt = jnp.concatenate([kc, kc], axis=0).T
            kt_s[hk * NC + c] = kt
            g = dot_wide(jnp.concatenate([kc, qc], axis=0), kt)
            gram_s[pl.ds((hk * NC + c) * CH, CH), :] = g[:CH]
            qk_s[hk * NC + c] = g[CH:]

    @pl.loop(0, CH, unroll=8)
    def _(i):
        x = gram_s[pl.ds(i, HK * NC, stride=CH), :]
        xt = jnp.concatenate([x, x], axis=0).T[:CH]
        keep = (start_s[...] == start_s[pl.ds(i, 1), :]) & (row_b < i)
        decay = jnp.exp(jnp.where(keep, cumt_s[pl.ds(i, 1), :] - cumt_s[...], -1e30))
        low_s[pl.ds(i * CH, CH), :] = xt * decay * bet_s[pl.ds(i, 1), :]

    for g in range(CH // 4):
        n = 8 * ((4 * g + 3) // 8 + 1)
        rid = lax.broadcasted_iota(jnp.int32, (n, D), 0)
        acc = tuple(jnp.where(rid == 4 * g + a, 1.0, 0.0).astype(F32) for a in range(4))

        def body(jb, acc, g=g, n=n):
            acc = list(acc)
            for b in range(4):
                t = inv_s[pl.ds((jb * 4 + b) * CH, n), :]
                for a in range(4):
                    acc[a] = acc[a] - low_s[pl.ds((4 * g + a) * CH + jb * 4 + b, 1), :] * t
            return tuple(acc)

        if g:
            acc = lax.fori_loop(0, g, body, acc)
        acc = list(acc)
        for a in range(4):
            for b in range(a):
                acc[a] = acc[a] - low_s[pl.ds((4 * g + a) * CH + 4 * g + b, 1), :] * acc[b]
            inv_s[pl.ds((4 * g + a) * CH, n), :] = acc[a]
            if n < CH:
                inv_s[pl.ds((4 * g + a) * CH + n, CH - n), :] = jnp.zeros((CH - n, D), F32)

    @pl.loop(0, CH, unroll=8)
    def _(i):
        x = inv_s[pl.ds(i * CH, CH), :] * bet_s[...]
        t_s[pl.ds(i, D, stride=CH), :] = jnp.concatenate([x, x], axis=0).T

    first_end = ends[-1]
    for e in ends[-2::-1]:
        first_end = jnp.where(e > off, e, first_end)
    marks = [first_end >= off + TOK]
    begin = 0
    for e in ends:
        marks.append((begin <= off) & (e > off) & (e <= off + TOK))
        begin = e
    mark = jnp.zeros((8, D), F32)
    for i, m in enumerate(marks):
        mark = jnp.where(row[:8] == i, jnp.where(m, 1.0, 0.0), mark)
    flag_ref[...] = mark

    eye = jnp.where(lane == row, 1.0, 0.0).astype(F32)
    zero = jnp.zeros((CH, D), F32)

    pairs = [(i, r) for i in range(NI) for r in range(2)]
    load_v.wait()

    def store(step):
        made = []
        at = pl.ds(step * 2 * NI, 2 * NI)
        for i, (a, b) in enumerate(((out0_ref, out0_hbm), (qe_ref, qe_hbm))):
            made.append(pltpu.make_async_copy(a.at[at], b.at[at], out_sem.at[step, i]))
        for j in range(4):
            for i, (a, b) in enumerate(((m1_ref, m1_hbm), (b1_ref, b1_hbm), (bo_ref, bo_hbm))):
                at = j * 8 + step
                made.append(pltpu.make_async_copy(a.at[at], b.at[at], out_sem.at[step, 2 + 3 * j + i]))
        return made

    @pl.loop(0, HK // NI)
    def _(step):
        hks = [step * NI + i for i in range(NI)]
        shift = lax.rem(D - step * (NI * NC), D)
        col_s[...] = pltpu.roll(cumt_s[...], shift, 1)
        gcol_s[...] = pltpu.roll(gamt_s[...], shift, 1)
        col = col_s[...]
        gcol = gcol_s[...]
        state = {}
        for c in range(NC):
            bias = bias_s[pl.ds(c * CH, CH), :]
            for i, r in pairs:
                hk = hks[i]
                h = hk * 2 + r
                kc = kn_s[hk, pl.ds(c * CH, CH), :]
                qc = qn_s[hk, pl.ds(c * CH, CH), :]
                kt = kt_s[hk * NC + c]
                qk = qk_s[hk * NC + c]
                at = r * CH + i * NC + c
                b = r * CH + hk * NC + c
                ccol = col[:, at : at + 1]
                gc = gcol[:, at : at + 1]
                decay = jnp.exp(ccol - cum_s[pl.ds(b, 1), :] + bias)
                v = v_ref[pl.ds(c * CH * H + h, CH, stride=H), :]
                gq = qc * gc
                uw = dot_twin(t_s[pl.ds(b * CH, CH), :], jnp.concatenate([v, kc * gc], axis=1))
                u0, w = uw[:, :D], uw[:, D:]
                if c == 0:
                    old = jnp.concatenate([jnp.zeros((D, D), F32), eye], axis=1)
                    u = jnp.concatenate([u0, -w], axis=1)
                    base = jnp.concatenate([zero, gq], axis=1)
                else:
                    old = state[i, r]
                    p = dot_wide(jnp.concatenate([w, gq], axis=0), old)
                    u = jnp.concatenate([u0, zero], axis=1) - p[:CH]
                    base = p[CH:]
                left = jnp.concatenate([qk * decay, kt * decay[CH - 1 : CH]], axis=0)
                res = dot_twin(left, u)
                o = base + res[:CH]
                out0_ref[h, pl.ds(c * CH, CH), :] = o[:, :D]
                qe_ref[h, pl.ds(c * CH, CH), :] = o[:, D:]
                st_s[i, r, c] = old
                u_s[i, r, c] = u
                state[i, r] = gc[CH - 1 : CH] * old + res[CH:]
        for i, r in pairs:
            h = hks[i] * 2 + r
            bo_ref[i * 16 + r * 8 + step] = state[i, r][:, :D]
            b1_ref[i * 16 + r * 8 + step] = state[i, r][:, :D]
            m1_ref[i * 16 + r * 8 + step] = state[i, r][:, D:]
        begin = 0
        for p in range(REQS):
            last = ends[p] - 1 - off
            here = (last >= 0) & (last < TOK)
            opens = begin <= off
            begin = ends[p]
            c = last // CH
            e = last % CH

            def scaled(i, r, c=c, e=e):
                at = lane[:1] == r * CH + i * NC + c
                crow = cum_s[pl.ds(r * CH + hks[i] * NC + c, 1), :]
                cume = jnp.sum(jnp.where(at, col_s[pl.ds(e, 1), :], 0.0), axis=1, keepdims=True)
                amp = jnp.sum(jnp.where(at, gcol_s[pl.ds(e, 1), :], 0.0), axis=1, keepdims=True)
                drow = jnp.exp(cume - crow + bias_s[pl.ds(c * CH + e, 1), :])
                return amp, kt_s[hks[i] * NC + c] * drow

            @pl.when(here & opens)
            def _(c=c, scaled=scaled):
                for i, r in pairs:
                    amp, kd = scaled(i, r)
                    f = amp * st_s[i, r, c] + dot_twin(kd, u_s[i, r, c])
                    b1_ref[i * 16 + r * 8 + step] = f[:, :D]
                    m1_ref[i * 16 + r * 8 + step] = f[:, D:]

            @pl.when(here & jnp.logical_not(opens))
            def _(c=c, p=p, scaled=scaled):
                for i, r in pairs:
                    amp, kd = scaled(i, r)
                    f = amp * st_s[i, r, c, :, :D] + dot_twin(kd, u_s[i, r, c, :, :D])
                    h = hks[i] * 2 + r
                    f0_ref[lax.rem(h, 4) * 2 + lax.rem(h // 4, 2), h // 8, p] = f.T

        for made in store(step):
            made.start()

    store_f0 = pltpu.make_async_copy(f0_ref, f0_hbm, in_sem.at[1])
    store_f0.start()

    @pl.loop(0, HK // NI)
    def _(step):
        for made in store(step):
            made.wait()

    store_f0.wait()


def local_terms(lengths, q, k, v, ld, be):
    hm = jax.ShapeDtypeStruct((H, D, D), F32)
    tokens = jax.ShapeDtypeStruct((H, TOK, D), F32)
    vm = pltpu.VMEM
    return pl.pallas_call(
        terms_kernel,
        out_shape=(
            tokens, tokens, hm, hm, hm,
            jax.ShapeDtypeStruct((8, 4, REQS, D, D), F32),
            jax.ShapeDtypeStruct((8, D), F32),
        ),
        in_specs=[SMEM, VMEM, VMEM, ANY, VMEM, VMEM],
        out_specs=tuple([ANY] * 6 + [VMEM]),
        scratch_shapes=[
            vm((H, TOK, D), F32),
            vm((H, TOK, D), F32),
            vm((H, D, D), F32),
            vm((H, D, D), F32),
            vm((H, D, D), F32),
            vm((8, 4, REQS, D, D), F32),
            vm((TOK * H, D), F32),
            pltpu.SemaphoreType.DMA((HK // NI, 14)),
            pltpu.SemaphoreType.DMA((2,)),
            vm((HK, TOK, D), F32),
            vm((HK, TOK, D), F32),
            vm((HK * NC, D, D), F32),
            vm((HK * NC * CH, D), F32),
            vm((HK * NC, CH, D), F32),
            vm((CH * CH, D), F32),
            vm((CH * CH, D), F32),
            vm((D * CH, D), F32),
            vm((D, D), F32),
            vm((D, D), F32),
            vm((CH, D), F32),
            vm((CH, D), F32),
            vm((CH, D), F32),
            vm((CH, D), jnp.int32),
            vm((TOK, D), F32),
            vm((CH, D), F32),
            vm((CH, D), F32),
            vm((NI, 2, NC, D, 2 * D), F32),
            vm((NI, 2, NC, CH, 2 * D), F32),
        ],
        compiler_params=pltpu.CompilerParams(vmem_limit_bytes=60 * 1024 * 1024),
        name="local_terms",
    )(lengths, q, k, v, ld, be)


def lines(me_ctx, me_grp):
    y, z = me_grp // 4, lax.rem(me_grp, 4)
    core = lax.rem(me_ctx, 2)

    def turn(i, by):
        return lax.rem(i + by, 4)

    return dict(
        twin={"ctx": me_ctx + 1 - 2 * core},
        chain={"ctx": lax.rem(me_ctx + 7 + 2 * core, 8)},
        x=({"ctx": lax.rem(me_ctx + 2, 8)}, {"ctx": lax.rem(me_ctx + 6, 8)}),
        z=({"grp": y * 4 + turn(z, 1)}, {"grp": y * 4 + turn(z, 3)}),
        y=({"grp": turn(y, 1) * 4 + z}, {"grp": turn(y, 3) * 4 + z}),
    )


class Copies:
    def __init__(self, send_sem, recv_sem):
        self.send_sem, self.recv_sem, self.made = send_sem, recv_sem, []

    def start(self, src, dst, device):
        i = len(self.made)
        made = pltpu.make_async_remote_copy(
            src_ref=src,
            dst_ref=dst,
            send_sem=self.send_sem.at[i],
            recv_sem=self.recv_sem.at[i],
            device_id=device,
            device_id_type=MESH,
        )
        made.start()
        self.made.append(made)
        return made

    def finish(self):
        for made in self.made:
            made.wait_send()


def add_units(dst, at, lo, n, src):
    for u in range(n):
        dst[at, lo + u] = dst[at, lo + u] + src[u]


def ring_ids(pos):
    return tuple(lax.rem(pos + i, 4) for i in (1, 2, 3))


def chain_kernel(
    own_ref, m_hbm, b1_hbm, bo_hbm, flag_ref, f0_hbm, in_ref, dec_ref,
    idx_ref, m_ref, b1_ref, bo_ref, load_sem, out_s, end_s, twin_s, xb, xc, xd, got_0, got_1, got_2, got_3, put_s, ya, yb, yc, yd,
    chain_send, chain_recv, send_sem, recv_sem,
):
    me = lax.axis_index("ctx")
    grp = lax.axis_index("grp")
    core, chip = lax.rem(me, 2), me // 2
    at = lines(me, grp)
    loads = []
    for j in range(4):
        rounds = [(a.at[pl.ds(8 * j, 8)], b.at[pl.ds(8 * j, 8)]) for a, b in
                  ((m_hbm, m_ref), (b1_hbm, b1_ref), (bo_hbm, bo_ref))]
        rounds.append((f0_hbm.at[pl.ds(2 * j, 2)], end_s.at[pl.ds(2 * j, 2)]))
        for i, (a, b) in enumerate(rounds):
            made = pltpu.make_async_copy(a, b, load_sem.at[4 * j + i])
            made.start()
            loads.append(made)

    y, z = grp // 4, lax.rem(grp, 4)
    for order in range(2):

        @pl.loop(0, 4)
        def _(t, order=order):
            line = (t * 4 + z) if order == 0 else (y * 4 + t)
            for slot in range(REQS):
                found = jnp.int32(-1)
                for i in range(16):
                    source = (y * 4 + i // 4) if order == 0 else ((i // 4) * 4 + z)
                    hit = own_ref[source * REQS + i % 4] == line * REQS + slot
                    found = jnp.where(hit, jnp.int32(i), found)
                idx_ref[order, t * REQS + slot] = found

    barrier = pltpu.get_barrier_semaphore()
    for device in (at["twin"], at["chain"], *at["x"], *at["y"], *at["z"]):
        pl.semaphore_signal(barrier, inc=1, device_id=device, device_id_type=MESH)
    pl.semaphore_wait(barrier, 8)
    copies = Copies(send_sem, recv_sem)
    got_s = (got_0, got_1, got_2, got_3)
    x_next, x_opp, x_prev = ring_ids(chip)
    x_up, x_down = at["x"]

    def pass_on(h):
        return pltpu.make_async_remote_copy(
            src_ref=out_s.at[h],
            dst_ref=in_ref.at[h],
            send_sem=chain_send.at[h],
            recv_sem=chain_recv.at[h],
            device_id={"ctx": lax.rem(me + 1, 8)},
            device_id_type=MESH,
        )

    @pl.when(me == 0)
    def _():
        @pl.loop(0, H)
        def _(h):
            in_ref[h] = jnp.zeros((D, D), F32)

    def advance(j):
        for made in loads[4 * j : 4 * j + 4]:
            made.wait()

        @pl.loop(0, 8)
        def _(e):
            h = e * 4 + j

            @pl.when(me > 0)
            def _():
                pass_on(h).wait_recv()

            x = dot_wide(m_ref[j * 8 + e], in_ref[h])
            out_s[h] = x * flag_ref[0:1, :] + bo_ref[j * 8 + e]

            @pl.when(me < 7)
            def _():
                pass_on(h).start()

            xt = (x + b1_ref[j * 8 + e]).T
            at, c = j * 2 + lax.rem(e, 2), e // 2
            for p in range(REQS):
                here = flag_ref[1 + p : 2 + p, :]
                end_s[at, c, p] = end_s[at, c, p] + here * xt

    twins, back, ahead, last = [], [], [], []

    def join(j):
        twins[j].wait_recv()

        @pl.loop(0, 4)
        def _(c):
            add_units(twin_s.at[j], c, 0, 4, end_s.at[j * 2 + core, c])

        back.append(copies.start(twin_s.at[j, x_opp], xb.at[j], x_down))

    def relay(j):
        back[j].wait_recv()
        add_units(twin_s.at[j], x_prev, 0, 4, xb.at[j])
        last.append(copies.start(twin_s.at[j, x_prev], xd.at[j], x_down))

    for j in range(4):
        advance(j)
        mine = end_s.at[j * 2 + 1 - core]
        twins.append(copies.start(mine, twin_s.at[j], at["twin"]))
        if j >= 1:
            join(j - 1)
    relay(0)
    ahead.append(copies.start(twin_s.at[0, x_next], xc.at[0], x_up))
    ahead.append(copies.start(twin_s.at[1, x_next], xc.at[1], x_up))
    join(3)
    relay(1)
    ahead.append(copies.start(twin_s.at[2, x_next], xc.at[2], x_up))
    ahead.append(copies.start(twin_s.at[3, x_next], xc.at[3], x_up))

    places = ((z, at["z"], y, at["y"]), (y, at["y"], z, at["z"]))
    direct, onward, begun, passed = [], [], [], []

    def spread(j):
        pos, (up, down), _, _ = places[j % 2]
        ahead[j].wait_recv()
        last[j].wait_recv()
        for u in range(4):
            got_s[j][pos * 4 + u] = twin_s[j, chip, u] + xc[j, u] + xd[j, u]
        mine = got_s[j].at[pl.ds(pos * 4, 4)]
        direct.append((copies.start(mine, mine, up), copies.start(mine, mine, down)))

    def forward(j):
        pos, (up, down), _, _ = places[j % 2]
        nxt, _, prv = ring_ids(pos)
        direct[j][0].wait_recv()
        part = got_s[j].at[pl.ds(prv * 4, 2)]
        c0 = copies.start(part, part, up)
        direct[j][1].wait_recv()
        part = got_s[j].at[pl.ds(nxt * 4 + 2, 2)]
        onward.append((c0, copies.start(part, part, down)))

    def pick(j):
        _, _, pos, (up, down) = places[j % 2]
        nxt, opp, prv = ring_ids(pos)
        onward[j][0].wait_recv()
        onward[j][1].wait_recv()

        @pl.loop(0, 4)
        def _(t):
            for s in range(REQS):
                src = idx_ref[j % 2, t * REQS + s]
                x = got_s[j][jnp.maximum(src, 0)]
                put_s[j * 4 + t, s] = jnp.where(src >= 0, x, 0.0)

        put = put_s.at[pl.ds(j * 4, 4)]
        c0 = copies.start(put.at[opp, pl.ds(0, 2)], ya.at[j], up)
        c1 = copies.start(put.at[opp, pl.ds(2, 2)], yb.at[j], down)
        c2 = copies.start(put.at[nxt, pl.ds(2, 2)], yc.at[j, pl.ds(2, 2)], up)
        c3 = copies.start(put.at[prv, pl.ds(0, 2)], yd.at[j, pl.ds(0, 2)], down)
        begun.append((c0, c1, c2, c3))

    def total(j):
        _, _, pos, (up, down) = places[j % 2]
        nxt, _, prv = ring_ids(pos)
        c0, c1, c2, c3 = begun[j]
        put = put_s.at[pl.ds(j * 4, 4)]
        c0.wait_recv()
        add_units(put, nxt, 0, 2, ya.at[j])
        c4 = copies.start(put.at[nxt, pl.ds(0, 2)], yc.at[j, pl.ds(0, 2)], up)
        c1.wait_recv()
        add_units(put, prv, 2, 2, yb.at[j])
        c5 = copies.start(put.at[prv, pl.ds(2, 2)], yd.at[j, pl.ds(2, 2)], down)
        passed.append((c2, c3, c4, c5))

    def settle(j):
        _, _, pos, _ = places[j % 2]
        for made in passed[j]:
            made.wait_recv()
        for s in range(REQS):
            dec_ref[s, j] = put_s[j * 4 + pos, s] + yc[j, s] + yd[j, s]

    spread(0)
    relay(2)
    spread(1)
    relay(3)
    forward(0)
    forward(1)
    spread(2)
    spread(3)
    pick(0)
    pick(1)
    forward(2)
    forward(3)
    total(0)
    total(1)
    pick(2)
    pick(3)
    settle(0)
    settle(1)
    total(2)
    total(3)
    settle(2)
    settle(3)

    @pl.when(me < 7)
    def _():
        @pl.loop(0, H)
        def _(h):
            pass_on(h).wait_send()

    copies.finish()


def chain(idx, m1, b1, bo, flag, f0):
    vm = pltpu.VMEM

    def units(*n):
        return vm(n + (D, D), F32)

    return pl.pallas_call(
        chain_kernel,
        out_shape=(
            jax.ShapeDtypeStruct((H, D, D), F32),
            jax.ShapeDtypeStruct((REQS, REQS, D, D), F32),
        ),
        in_specs=[SMEM, ANY, ANY, ANY, VMEM, ANY],
        out_specs=(VMEM, VMEM),
        scratch_shapes=[
            pltpu.SMEM((2, 16), jnp.int32),
            units(H), units(H), units(H), pltpu.SemaphoreType.DMA((16,)),
            units(H), units(8, 4, 4), units(4, 4, 4),
            units(4, 4), units(4, 4), units(4, 4),
            units(16), units(16), units(16), units(16), units(16, 4),
            units(4, 2), units(4, 2), units(4, 4), units(4, 4),
            pltpu.SemaphoreType.DMA((H,)),
            pltpu.SemaphoreType.DMA((H,)),
            pltpu.SemaphoreType.DMA((64,)),
            pltpu.SemaphoreType.DMA((64,)),
        ],
        compiler_params=pltpu.CompilerParams(
            collective_id=0, has_side_effects=True, vmem_limit_bytes=60 * 1024 * 1024
        ),
        name="state_chain",
    )(idx, m1, b1, bo, flag, f0)


HB = 8


def gate_kernel(out0_ref, qe_ref, x_ref, gate_ref, gain_ref, o_ref):
    gain = gain_ref[...]
    gate = gate_ref.reshape(TOK * HB, D)
    dst = o_ref.reshape(TOK * HB, D)
    for h in range(HB):
        raw = out0_ref[h] + dot_wide(qe_ref[h], x_ref[h])
        ms = jnp.sum(raw * raw, axis=1, keepdims=True) * (1.0 / D)
        g = gate[pl.ds(h, TOK, stride=HB), :]
        act = g / (1.0 + jnp.exp(-g))
        dst[pl.ds(h, TOK, stride=HB), :] = raw * lax.rsqrt(ms + 1e-6) * gain * act


def gated_out(out0, qe, x_in, gate, gain):
    tok = pl.BlockSpec((HB, TOK, D), lambda i: (i, 0, 0))
    nat = pl.BlockSpec((TOK, HB, D), lambda i: (0, i, 0))
    return pl.pallas_call(
        gate_kernel,
        grid=(H // HB,),
        out_shape=jax.ShapeDtypeStruct((TOK, H, D), F32),
        in_specs=[
            tok, tok,
            pl.BlockSpec((HB, D, D), lambda i: (i, 0, 0)),
            nat,
            pl.BlockSpec((1, D), lambda i: (0, 0)),
        ],
        out_specs=nat,
        compiler_params=pltpu.CompilerParams(vmem_limit_bytes=60 * 1024 * 1024),
        cost_estimate=pl.CostEstimate(flops=800000000, bytes_accessed=20000000, transcendentals=0),
        name="gated_out",
    )(out0, qe, x_in, gate, gain)


def local(
    queries, key_vecs, val_vecs, out_gate, log_decay, beta_gate, norm_gain, lengths, owner_slot
):
    out0, qe, m1, b1, bo, f0, flag = local_terms(
        lengths,
        queries.reshape(TOK * HK, D),
        key_vecs.reshape(TOK * HK, D),
        val_vecs.reshape(TOK * H, D),
        log_decay[0],
        beta_gate[0],
    )
    x_in, decode = chain(owner_slot, m1, b1, bo, flag, f0)
    attn = gated_out(out0, qe, x_in, out_gate[0], norm_gain.reshape(1, D))
    return attn[None], decode


def solution(mesh):
    return jax.shard_map(
        local,
        mesh=mesh,
        in_specs=(
            P("grp", "ctx", None, None),
            P("grp", "ctx", None, None),
            P("grp", "ctx", None, None),
            P("grp", "ctx", None, None),
            P("grp", None, "ctx"),
            P("grp", None, "ctx"),
            P(),
            P("grp", None),
            P(),
        ),
        out_specs=(P("grp", "ctx", None, None), P("grp", "ctx", None, None)),
        check_vma=False,
    )
```

```python
import jax
import jax.numpy as jnp
from jax import lax
from jax.experimental import pallas as pl
from jax.experimental.pallas import tpu as pltpu
from jax.sharding import PartitionSpec as P

CH = 64
D = 128
HK = 16
H = 32
TOK = 256
NC = TOK // CH
REQS = 4
NI = 2
F32 = jnp.float32
BF16 = jnp.bfloat16
MESH = pl.DeviceIdType.MESH
VMEM = pl.BlockSpec(memory_space=pltpu.VMEM)
SMEM = pl.BlockSpec(memory_space=pltpu.SMEM)
ANY = pl.BlockSpec(memory_space=pl.ANY)


def mm(x, y):
    return lax.dot_general(x, y, (((1,), (0,)), ((), ())), preferred_element_type=F32)


def split(x):
    hi = x.astype(BF16)
    return hi, (x - hi.astype(F32)).astype(BF16)


def dot_wide(x, y):
    xh, xl = split(x)
    yh, yl = split(y)
    left = jnp.concatenate([xh, xl], axis=1)
    return mm(left, jnp.concatenate([yh, yh], axis=0)) + mm(xh, yl)


def dot_twin(x, y):
    low = x - x.astype(BF16).astype(F32)
    lane = lax.broadcasted_iota(jnp.int32, x.shape, 1)
    s = jnp.where(lane < CH, x, low).astype(BF16)
    yh, yl = split(y)
    left = jnp.concatenate([s, s], axis=1)
    return mm(left, jnp.concatenate([yh, yh, yl, yl], axis=0))


def prompt_ends(len_ref):
    ends = [len_ref[0, 0]]
    for r in range(1, REQS):
        ends.append(ends[-1] + len_ref[0, r])
    return ends


def seg_start(pos, ends):
    start = jnp.zeros(pos.shape, jnp.int32)
    for e in ends[:-1]:
        start = jnp.where(pos >= e, e, start)
    return start


def terms_kernel(
    len_ref, q_ref, k_ref, v_hbm, ld_ref, be_ref,
    out0_hbm, qe_hbm, m1_hbm, b1_hbm, bo_hbm, f0_hbm, flag_ref,
    out0_ref, qe_ref, m1_ref, b1_ref, bo_ref, f0_ref, v_ref, out_sem, in_sem,
    kn_s, qn_s, kt_s, gram_s, qk_s, low_s, inv_s, t_s,
    cum_s, gam_s, cumt_s, gamt_s, bet_s, start_s, bias_s, col_s, gcol_s, st_s, u_s,
):
    load_v = pltpu.make_async_copy(v_hbm, v_ref, in_sem.at[0])
    load_v.start()
    off = lax.axis_index("ctx") * TOK
    ends = prompt_ends(len_ref)
    lane = lax.broadcasted_iota(jnp.int32, (D, D), 1)
    row = lax.broadcasted_iota(jnp.int32, (D, D), 0)

    tok = lane % CH
    for i, src in enumerate((ld_ref, be_ref)):
        x = src[...]
        low_s[2 * i * H : (2 * i + 1) * H, :] = x[:, :D]
        low_s[(2 * i + 1) * H : (2 * i + 2) * H, :] = x[:, D:]
    for c in range(NC):
        for r in range(2):
            for i, dst in enumerate((cum_s, gam_s)):
                x = low_s[pl.ds((2 * i + c // 2) * H + r, HK, stride=2), :]
                y = pltpu.roll(x, CH, 1)
                x = jnp.where((lane[:HK] < CH) == (c % 2 == 0), x, y)
                dst[pl.ds(r * CH + c, HK, stride=NC), :] = x
    cum = cum_s[...]
    beta = gam_s[...]
    for s in (1, 2, 4, 8, 16, 32):
        cum = cum + jnp.where(tok >= s, pltpu.roll(cum, s, 1), 0.0)
    lo_a = off + (row % NC) * CH
    carry_a = seg_start(lo_a + tok, ends) < lo_a
    gam = jnp.where(carry_a, jnp.exp(cum), 0.0)
    cum_s[...] = cum
    gam_s[...] = gam
    cumt_s[...] = cum.T[:CH]
    gamt_s[...] = gam.T[:CH]
    bet_s[...] = beta.T[:CH]
    lane_b = lane[:CH]
    row_b = row[:CH]
    start_s[...] = seg_start(off + (lane_b % NC) * CH + row_b, ends)
    tok_b = tok[:CH]
    for c in range(NC):
        lo = off + c * CH
        same = seg_start(lo + row_b, ends) == seg_start(lo + tok_b, ends)
        bias_s[pl.ds(c * CH, CH), :] = jnp.where(same & (tok_b <= row_b), 0.0, -1e30)

    @pl.loop(0, 8)
    def _(i):
        for u in range(16):
            f0_ref[i, u // 4, u % 4] = jnp.zeros((D, D), F32)

    @pl.loop(0, HK, unroll=4)
    def _(hk):
        k = k_ref[pl.ds(hk, TOK, stride=HK), :]
        q = q_ref[pl.ds(hk, TOK, stride=HK), :]
        kn = k * lax.rsqrt(jnp.sum(k * k, axis=1, keepdims=True) + 1e-6)
        qn = q * (lax.rsqrt(jnp.sum(q * q, axis=1, keepdims=True) + 1e-6) * (D**-0.5))
        kn_s[hk] = kn
        qn_s[hk] = qn
        for c in range(NC):
            kc = kn[c * CH : (c + 1) * CH]
            qc = qn[c * CH : (c + 1) * CH]
            kt = jnp.concatenate([kc, kc], axis=0).T
            kt_s[hk * NC + c] = kt
            g = dot_wide(jnp.concatenate([kc, qc], axis=0), kt)
            gram_s[pl.ds((hk * NC + c) * CH, CH), :] = g[:CH]
            qk_s[hk * NC + c] = g[CH:]

    @pl.loop(0, CH, unroll=8)
    def _(i):
        x = gram_s[pl.ds(i, HK * NC, stride=CH), :]
        xt = jnp.concatenate([x, x], axis=0).T[:CH]
        keep = (start_s[...] == start_s[pl.ds(i, 1), :]) & (row_b < i)
        decay = jnp.exp(jnp.where(keep, cumt_s[pl.ds(i, 1), :] - cumt_s[...], -1e30))
        low_s[pl.ds(i * CH, CH), :] = xt * decay * bet_s[pl.ds(i, 1), :]

    for g in range(CH // 4):
        n = 8 * ((4 * g + 3) // 8 + 1)
        rid = lax.broadcasted_iota(jnp.int32, (n, D), 0)
        acc = tuple(jnp.where(rid == 4 * g + a, 1.0, 0.0).astype(F32) for a in range(4))

        def body(jb, acc, g=g, n=n):
            acc = list(acc)
            for b in range(4):
                t = inv_s[pl.ds((jb * 4 + b) * CH, n), :]
                for a in range(4):
                    acc[a] = acc[a] - low_s[pl.ds((4 * g + a) * CH + jb * 4 + b, 1), :] * t
            return tuple(acc)

        if g:
            acc = lax.fori_loop(0, g, body, acc)
        acc = list(acc)
        for a in range(4):
            for b in range(a):
                acc[a] = acc[a] - low_s[pl.ds((4 * g + a) * CH + 4 * g + b, 1), :] * acc[b]
            inv_s[pl.ds((4 * g + a) * CH, n), :] = acc[a]
            if n < CH:
                inv_s[pl.ds((4 * g + a) * CH + n, CH - n), :] = jnp.zeros((CH - n, D), F32)

    @pl.loop(0, CH, unroll=8)
    def _(i):
        x = inv_s[pl.ds(i * CH, CH), :] * bet_s[...]
        t_s[pl.ds(i, D, stride=CH), :] = jnp.concatenate([x, x], axis=0).T

    first_end = ends[-1]
    for e in ends[-2::-1]:
        first_end = jnp.where(e > off, e, first_end)
    marks = [first_end >= off + TOK]
    begin = 0
    for e in ends:
        marks.append((begin <= off) & (e > off) & (e <= off + TOK))
        begin = e
    mark = jnp.zeros((8, D), F32)
    for i, m in enumerate(marks):
        mark = jnp.where(row[:8] == i, jnp.where(m, 1.0, 0.0), mark)
    flag_ref[...] = mark

    eye = jnp.where(lane == row, 1.0, 0.0).astype(F32)
    zero = jnp.zeros((CH, D), F32)

    pairs = [(i, r) for i in range(NI) for r in range(2)]
    load_v.wait()

    def store(step):
        made = []
        at = pl.ds(step * 2 * NI, 2 * NI)
        for i, (a, b) in enumerate(((out0_ref, out0_hbm), (qe_ref, qe_hbm))):
            made.append(pltpu.make_async_copy(a.at[at], b.at[at], out_sem.at[step, i]))
        for j in range(4):
            for i, (a, b) in enumerate(((m1_ref, m1_hbm), (b1_ref, b1_hbm), (bo_ref, bo_hbm))):
                at = j * 8 + step
                made.append(pltpu.make_async_copy(a.at[at], b.at[at], out_sem.at[step, 2 + 3 * j + i]))
        return made

    @pl.loop(0, HK // NI)
    def _(step):
        hks = [step * NI + i for i in range(NI)]
        shift = lax.rem(D - step * (NI * NC), D)
        col_s[...] = pltpu.roll(cumt_s[...], shift, 1)
        gcol_s[...] = pltpu.roll(gamt_s[...], shift, 1)
        col = col_s[...]
        gcol = gcol_s[...]
        state = {}
        for c in range(NC):
            bias = bias_s[pl.ds(c * CH, CH), :]
            for i, r in pairs:
                hk = hks[i]
                h = hk * 2 + r
                kc = kn_s[hk, pl.ds(c * CH, CH), :]
                qc = qn_s[hk, pl.ds(c * CH, CH), :]
                kt = kt_s[hk * NC + c]
                qk = qk_s[hk * NC + c]
                at = r * CH + i * NC + c
                b = r * CH + hk * NC + c
                ccol = col[:, at : at + 1]
                gc = gcol[:, at : at + 1]
                decay = jnp.exp(ccol - cum_s[pl.ds(b, 1), :] + bias)
                v = v_ref[pl.ds(c * CH * H + h, CH, stride=H), :]
                gq = qc * gc
                uw = dot_twin(t_s[pl.ds(b * CH, CH), :], jnp.concatenate([v, kc * gc], axis=1))
                u0, w = uw[:, :D], uw[:, D:]
                if c == 0:
                    old = jnp.concatenate([jnp.zeros((D, D), F32), eye], axis=1)
                    u = jnp.concatenate([u0, -w], axis=1)
                    base = jnp.concatenate([zero, gq], axis=1)
                else:
                    old = state[i, r]
                    p = dot_wide(jnp.concatenate([w, gq], axis=0), old)
                    u = jnp.concatenate([u0, zero], axis=1) - p[:CH]
                    base = p[CH:]
                left = jnp.concatenate([qk * decay, kt * decay[CH - 1 : CH]], axis=0)
                res = dot_twin(left, u)
                o = base + res[:CH]
                out0_ref[h, pl.ds(c * CH, CH), :] = o[:, :D]
                qe_ref[h, pl.ds(c * CH, CH), :] = o[:, D:]
                st_s[i, r, c] = old
                u_s[i, r, c] = u
                state[i, r] = gc[CH - 1 : CH] * old + res[CH:]
        for i, r in pairs:
            h = hks[i] * 2 + r
            bo_ref[i * 16 + r * 8 + step] = state[i, r][:, :D]
            b1_ref[i * 16 + r * 8 + step] = state[i, r][:, :D]
            m1_ref[i * 16 + r * 8 + step] = state[i, r][:, D:]
        begin = 0
        for p in range(REQS):
            last = ends[p] - 1 - off
            here = (last >= 0) & (last < TOK)
            opens = begin <= off
            begin = ends[p]
            c = last // CH
            e = last % CH

            def scaled(i, r, c=c, e=e):
                at = lane[:1] == r * CH + i * NC + c
                crow = cum_s[pl.ds(r * CH + hks[i] * NC + c, 1), :]
                cume = jnp.sum(jnp.where(at, col_s[pl.ds(e, 1), :], 0.0), axis=1, keepdims=True)
                amp = jnp.sum(jnp.where(at, gcol_s[pl.ds(e, 1), :], 0.0), axis=1, keepdims=True)
                drow = jnp.exp(cume - crow + bias_s[pl.ds(c * CH + e, 1), :])
                return amp, kt_s[hks[i] * NC + c] * drow

            @pl.when(here & opens)
            def _(c=c, scaled=scaled):
                for i, r in pairs:
                    amp, kd = scaled(i, r)
                    f = amp * st_s[i, r, c] + dot_twin(kd, u_s[i, r, c])
                    b1_ref[i * 16 + r * 8 + step] = f[:, :D]
                    m1_ref[i * 16 + r * 8 + step] = f[:, D:]

            @pl.when(here & jnp.logical_not(opens))
            def _(c=c, p=p, scaled=scaled):
                for i, r in pairs:
                    amp, kd = scaled(i, r)
                    f = amp * st_s[i, r, c, :, :D] + dot_twin(kd, u_s[i, r, c, :, :D])
                    h = hks[i] * 2 + r
                    f0_ref[lax.rem(h, 4) * 2 + lax.rem(h // 4, 2), h // 8, p] = f.T

        for made in store(step):
            made.start()

    store_f0 = pltpu.make_async_copy(f0_ref, f0_hbm, in_sem.at[1])
    store_f0.start()

    @pl.loop(0, HK // NI)
    def _(step):
        for made in store(step):
            made.wait()

    store_f0.wait()


def local_terms(lengths, q, k, v, ld, be):
    hm = jax.ShapeDtypeStruct((H, D, D), F32)
    tokens = jax.ShapeDtypeStruct((H, TOK, D), F32)
    vm = pltpu.VMEM
    return pl.pallas_call(
        terms_kernel,
        out_shape=(
            tokens, tokens, hm, hm, hm,
            jax.ShapeDtypeStruct((8, 4, REQS, D, D), F32),
            jax.ShapeDtypeStruct((8, D), F32),
        ),
        in_specs=[SMEM, VMEM, VMEM, ANY, VMEM, VMEM],
        out_specs=tuple([ANY] * 6 + [VMEM]),
        scratch_shapes=[
            vm((H, TOK, D), F32),
            vm((H, TOK, D), F32),
            vm((H, D, D), F32),
            vm((H, D, D), F32),
            vm((H, D, D), F32),
            vm((8, 4, REQS, D, D), F32),
            vm((TOK * H, D), F32),
            pltpu.SemaphoreType.DMA((HK // NI, 14)),
            pltpu.SemaphoreType.DMA((2,)),
            vm((HK, TOK, D), F32),
            vm((HK, TOK, D), F32),
            vm((HK * NC, D, D), F32),
            vm((HK * NC * CH, D), F32),
            vm((HK * NC, CH, D), F32),
            vm((CH * CH, D), F32),
            vm((CH * CH, D), F32),
            vm((D * CH, D), F32),
            vm((D, D), F32),
            vm((D, D), F32),
            vm((CH, D), F32),
            vm((CH, D), F32),
            vm((CH, D), F32),
            vm((CH, D), jnp.int32),
            vm((TOK, D), F32),
            vm((CH, D), F32),
            vm((CH, D), F32),
            vm((NI, 2, NC, D, 2 * D), F32),
            vm((NI, 2, NC, CH, 2 * D), F32),
        ],
        compiler_params=pltpu.CompilerParams(vmem_limit_bytes=60 * 1024 * 1024),
        name="local_terms",
    )(lengths, q, k, v, ld, be)


def lines(me_ctx, me_grp):
    y, z = me_grp // 4, lax.rem(me_grp, 4)
    core = lax.rem(me_ctx, 2)

    def turn(i, by):
        return lax.rem(i + by, 4)

    return dict(
        twin={"ctx": me_ctx + 1 - 2 * core},
        chain={"ctx": lax.rem(me_ctx + 7 + 2 * core, 8)},
        x=({"ctx": lax.rem(me_ctx + 2, 8)}, {"ctx": lax.rem(me_ctx + 6, 8)}),
        z=({"grp": y * 4 + turn(z, 1)}, {"grp": y * 4 + turn(z, 3)}),
        y=({"grp": turn(y, 1) * 4 + z}, {"grp": turn(y, 3) * 4 + z}),
    )


class Copies:
    def __init__(self, send_sem, recv_sem):
        self.send_sem, self.recv_sem, self.made = send_sem, recv_sem, []

    def start(self, src, dst, device):
        i = len(self.made)
        made = pltpu.make_async_remote_copy(
            src_ref=src,
            dst_ref=dst,
            send_sem=self.send_sem.at[i],
            recv_sem=self.recv_sem.at[i],
            device_id=device,
            device_id_type=MESH,
        )
        made.start()
        self.made.append(made)
        return made

    def finish(self):
        for made in self.made:
            made.wait_send()


def add_units(dst, at, lo, n, src):
    for u in range(n):
        dst[at, lo + u] = dst[at, lo + u] + src[u]


def ring_ids(pos):
    return tuple(lax.rem(pos + i, 4) for i in (1, 2, 3))


def chain_kernel(
    own_ref, m_hbm, b1_hbm, bo_hbm, flag_ref, f0_hbm, in_ref, dec_ref,
    idx_ref, m_ref, b1_ref, bo_ref, load_sem, out_s, end_s, twin_s, xb, xc, xd, got_0, got_1, got_2, got_3, put_s, ya, yb, yc, yd,
    chain_send, chain_recv, send_sem, recv_sem,
):
    me = lax.axis_index("ctx")
    grp = lax.axis_index("grp")
    core, chip = lax.rem(me, 2), me // 2
    at = lines(me, grp)
    loads = []
    for j in range(4):
        rounds = [(a.at[pl.ds(8 * j, 8)], b.at[pl.ds(8 * j, 8)]) for a, b in
                  ((m_hbm, m_ref), (b1_hbm, b1_ref), (bo_hbm, bo_ref))]
        rounds.append((f0_hbm.at[pl.ds(2 * j, 2)], end_s.at[pl.ds(2 * j, 2)]))
        for i, (a, b) in enumerate(rounds):
            made = pltpu.make_async_copy(a, b, load_sem.at[4 * j + i])
            made.start()
            loads.append(made)

    y, z = grp // 4, lax.rem(grp, 4)
    for order in range(2):

        @pl.loop(0, 4)
        def _(t, order=order):
            line = (t * 4 + z) if order == 0 else (y * 4 + t)
            for slot in range(REQS):
                found = jnp.int32(-1)
                for i in range(16):
                    source = (y * 4 + i // 4) if order == 0 else ((i // 4) * 4 + z)
                    hit = own_ref[source * REQS + i % 4] == line * REQS + slot
                    found = jnp.where(hit, jnp.int32(i), found)
                idx_ref[order, t * REQS + slot] = found

    barrier = pltpu.get_barrier_semaphore()
    for device in (at["twin"], at["chain"], *at["x"], *at["y"], *at["z"]):
        pl.semaphore_signal(barrier, inc=1, device_id=device, device_id_type=MESH)
    pl.semaphore_wait(barrier, 8)
    copies = Copies(send_sem, recv_sem)
    got_s = (got_0, got_1, got_2, got_3)
    x_next, x_opp, x_prev = ring_ids(chip)
    x_up, x_down = at["x"]

    def pass_on(h):
        return pltpu.make_async_remote_copy(
            src_ref=out_s.at[h],
            dst_ref=in_ref.at[h],
            send_sem=chain_send.at[h],
            recv_sem=chain_recv.at[h],
            device_id={"ctx": lax.rem(me + 1, 8)},
            device_id_type=MESH,
        )

    @pl.when(me == 0)
    def _():
        @pl.loop(0, H)
        def _(h):
            in_ref[h] = jnp.zeros((D, D), F32)

    def advance(j):
        for made in loads[4 * j : 4 * j + 4]:
            made.wait()

        @pl.loop(0, 8)
        def _(e):
            h = e * 4 + j

            @pl.when(me > 0)
            def _():
                pass_on(h).wait_recv()

            x = dot_wide(m_ref[j * 8 + e], in_ref[h])
            out_s[h] = x * flag_ref[0:1, :] + bo_ref[j * 8 + e]

            @pl.when(me < 7)
            def _():
                pass_on(h).start()

            xt = (x + b1_ref[j * 8 + e]).T
            at, c = j * 2 + lax.rem(e, 2), e // 2
            for p in range(REQS):
                here = flag_ref[1 + p : 2 + p, :]
                end_s[at, c, p] = end_s[at, c, p] + here * xt

    twins, back, ahead, last = [], [], [], []
    span = pl.ds(chip // 2, 3)

    def add_span(j, at, sender, src):
        lo = sender // 2
        for u in range(3):
            twin_s[j, at, lo + u] = twin_s[j, at, lo + u] + src[j, lo + u]

    def join(j):
        twins[j].wait_recv()

        @pl.loop(0, 4)
        def _(c):
            add_units(twin_s.at[j], c, 0, 4, end_s.at[j * 2 + core, c])

        back.append(copies.start(twin_s.at[j, x_opp, span], xb.at[j, span], x_down))

    def relay(j):
        back[j].wait_recv()
        add_span(j, x_prev, x_next, xb)
        last.append(copies.start(twin_s.at[j, x_prev], xd.at[j], x_down))

    for j in range(4):
        advance(j)
        mine = end_s.at[j * 2 + 1 - core]
        twins.append(copies.start(mine, twin_s.at[j], at["twin"]))
        if j >= 1:
            join(j - 1)
    relay(0)
    ahead.append(copies.start(twin_s.at[0, x_next, span], xc.at[0, span], x_up))
    ahead.append(copies.start(twin_s.at[1, x_next, span], xc.at[1, span], x_up))
    join(3)
    relay(1)
    ahead.append(copies.start(twin_s.at[2, x_next, span], xc.at[2, span], x_up))
    ahead.append(copies.start(twin_s.at[3, x_next, span], xc.at[3, span], x_up))

    places = ((z, at["z"], y, at["y"]), (y, at["y"], z, at["z"]))
    direct, onward, begun, passed = [], [], [], []

    def spread(j):
        pos, (up, down), _, _ = places[j % 2]
        ahead[j].wait_recv()
        last[j].wait_recv()
        add_span(j, chip, x_prev, xc)
        for u in range(4):
            got_s[j][pos * 4 + u] = twin_s[j, chip, u] + xd[j, u]
        mine = got_s[j].at[pl.ds(pos * 4, 4)]
        direct.append((copies.start(mine, mine, up), copies.start(mine, mine, down)))

    def forward(j):
        pos, (up, down), _, _ = places[j % 2]
        nxt, _, prv = ring_ids(pos)
        direct[j][0].wait_recv()
        part = got_s[j].at[pl.ds(prv * 4, 2)]
        c0 = copies.start(part, part, up)
        direct[j][1].wait_recv()
        part = got_s[j].at[pl.ds(nxt * 4 + 2, 2)]
        onward.append((c0, copies.start(part, part, down)))

    def pick(j):
        _, _, pos, (up, down) = places[j % 2]
        nxt, opp, prv = ring_ids(pos)
        onward[j][0].wait_recv()
        onward[j][1].wait_recv()

        @pl.loop(0, 4)
        def _(t):
            for s in range(REQS):
                src = idx_ref[j % 2, t * REQS + s]
                x = got_s[j][jnp.maximum(src, 0)]
                put_s[j * 4 + t, s] = jnp.where(src >= 0, x, 0.0)

        put = put_s.at[pl.ds(j * 4, 4)]
        c0 = copies.start(put.at[opp, pl.ds(0, 2)], ya.at[j], up)
        c1 = copies.start(put.at[opp, pl.ds(2, 2)], yb.at[j], down)
        c2 = copies.start(put.at[nxt, pl.ds(2, 2)], yc.at[j, pl.ds(2, 2)], up)
        c3 = copies.start(put.at[prv, pl.ds(0, 2)], yd.at[j, pl.ds(0, 2)], down)
        begun.append((c0, c1, c2, c3))

    def total(j):
        _, _, pos, (up, down) = places[j % 2]
        nxt, _, prv = ring_ids(pos)
        c0, c1, c2, c3 = begun[j]
        put = put_s.at[pl.ds(j * 4, 4)]
        c0.wait_recv()
        add_units(put, nxt, 0, 2, ya.at[j])
        c4 = copies.start(put.at[nxt, pl.ds(0, 2)], yc.at[j, pl.ds(0, 2)], up)
        c1.wait_recv()
        add_units(put, prv, 2, 2, yb.at[j])
        c5 = copies.start(put.at[prv, pl.ds(2, 2)], yd.at[j, pl.ds(2, 2)], down)
        passed.append((c2, c3, c4, c5))

    def settle(j):
        _, _, pos, _ = places[j % 2]
        for made in passed[j]:
            made.wait_recv()
        for s in range(REQS):
            dec_ref[s, j] = put_s[j * 4 + pos, s] + yc[j, s] + yd[j, s]

    spread(0)
    relay(2)
    spread(1)
    relay(3)
    forward(0)
    forward(1)
    spread(2)
    spread(3)
    pick(0)
    pick(1)
    forward(2)
    forward(3)
    total(0)
    total(1)
    pick(2)
    pick(3)
    settle(0)
    settle(1)
    total(2)
    total(3)
    settle(2)
    settle(3)

    @pl.when(me < 7)
    def _():
        @pl.loop(0, H)
        def _(h):
            pass_on(h).wait_send()

    copies.finish()


def chain(idx, m1, b1, bo, flag, f0):
    vm = pltpu.VMEM

    def units(*n):
        return vm(n + (D, D), F32)

    return pl.pallas_call(
        chain_kernel,
        out_shape=(
            jax.ShapeDtypeStruct((H, D, D), F32),
            jax.ShapeDtypeStruct((REQS, REQS, D, D), F32),
        ),
        in_specs=[SMEM, ANY, ANY, ANY, VMEM, ANY],
        out_specs=(VMEM, VMEM),
        scratch_shapes=[
            pltpu.SMEM((2, 16), jnp.int32),
            units(H), units(H), units(H), pltpu.SemaphoreType.DMA((16,)),
            units(H), units(8, 4, 4), units(4, 4, 4),
            units(4, 4), units(4, 4), units(4, 4),
            units(16), units(16), units(16), units(16), units(16, 4),
            units(4, 2), units(4, 2), units(4, 4), units(4, 4),
            pltpu.SemaphoreType.DMA((H,)),
            pltpu.SemaphoreType.DMA((H,)),
            pltpu.SemaphoreType.DMA((64,)),
            pltpu.SemaphoreType.DMA((64,)),
        ],
        compiler_params=pltpu.CompilerParams(
            collective_id=0, has_side_effects=True, vmem_limit_bytes=60 * 1024 * 1024
        ),
        name="state_chain",
    )(idx, m1, b1, bo, flag, f0)


HB = 8


def gate_kernel(out0_ref, qe_ref, x_ref, gate_ref, gain_ref, o_ref):
    gain = gain_ref[...]
    gate = gate_ref.reshape(TOK * HB, D)
    dst = o_ref.reshape(TOK * HB, D)
    for h in range(HB):
        raw = out0_ref[h] + dot_wide(qe_ref[h], x_ref[h])
        ms = jnp.sum(raw * raw, axis=1, keepdims=True) * (1.0 / D)
        g = gate[pl.ds(h, TOK, stride=HB), :]
        act = g / (1.0 + jnp.exp(-g))
        dst[pl.ds(h, TOK, stride=HB), :] = raw * lax.rsqrt(ms + 1e-6) * gain * act


def gated_out(out0, qe, x_in, gate, gain):
    tok = pl.BlockSpec((HB, TOK, D), lambda i: (i, 0, 0))
    nat = pl.BlockSpec((TOK, HB, D), lambda i: (0, i, 0))
    return pl.pallas_call(
        gate_kernel,
        grid=(H // HB,),
        out_shape=jax.ShapeDtypeStruct((TOK, H, D), F32),
        in_specs=[
            tok, tok,
            pl.BlockSpec((HB, D, D), lambda i: (i, 0, 0)),
            nat,
            pl.BlockSpec((1, D), lambda i: (0, 0)),
        ],
        out_specs=nat,
        compiler_params=pltpu.CompilerParams(vmem_limit_bytes=60 * 1024 * 1024),
        cost_estimate=pl.CostEstimate(flops=800000000, bytes_accessed=20000000, transcendentals=0),
        name="gated_out",
    )(out0, qe, x_in, gate, gain)


def local(
    queries, key_vecs, val_vecs, out_gate, log_decay, beta_gate, norm_gain, lengths, owner_slot
):
    out0, qe, m1, b1, bo, f0, flag = local_terms(
        lengths,
        queries.reshape(TOK * HK, D),
        key_vecs.reshape(TOK * HK, D),
        val_vecs.reshape(TOK * H, D),
        log_decay[0],
        beta_gate[0],
    )
    x_in, decode = chain(owner_slot, m1, b1, bo, flag, f0)
    attn = gated_out(out0, qe, x_in, out_gate[0], norm_gain.reshape(1, D))
    return attn[None], decode


def solution(mesh):
    return jax.shard_map(
        local,
        mesh=mesh,
        in_specs=(
            P("grp", "ctx", None, None),
            P("grp", "ctx", None, None),
            P("grp", "ctx", None, None),
            P("grp", "ctx", None, None),
            P("grp", None, "ctx"),
            P("grp", None, "ctx"),
            P(),
            P("grp", None),
            P(),
        ),
        out_specs=(P("grp", "ctx", None, None), P("grp", "ctx", None, None)),
        check_vma=False,
    )
```
